512 devices in a mesh: group: 2 (over x_hi), dp: 256 (over y, x_lo, z, core).
Axes of the slice: x: 4 (x_hi: 2, x_lo: 2; x = x_hi * 2 + x_lo), y: 8, z: 8, core: 2. Of those that a mesh axis runs over, the one named last changes fastest.
Arguments:
- operands: bfloat16 [2, 256, 256, 4096], P('group', 'dp'), may hold values from -32 to 32
Outputs:
- results: bfloat16 [2, 256, 256, 4096], P('group', 'dp')
The draws below stay inside these ranges and needn't reach their ends.
All inputs are finite; a program needn't handle non-finite values.
Results may differ from the reference program's by a relative error of at most 0.013.
Values may be sent and summed in bfloat16 or wider, within the bound.
No kernel may reach another device: no remote copies, remote signals or barrier semaphores. Data moves between devices by JAX's collectives and lax.ppermute only.
A program may use at most 64 MiB of HBM per device.

```python
import jax
import jax.numpy as jnp
from jax import lax

HEADS = 8
HEAD = 256
ROWS = 256
INNER = 2048
SEQS = 256
N_GROUP = 2


def draw_operands(key, part):
    key = jax.random.fold_in(key, 11)
    first_key = jax.random.fold_in(key, 0)
    full_shape = (N_GROUP, SEQS, ROWS, 2 * INNER)
    sample = jnp.clip(jax.random.normal(first_key, full_shape, jnp.float32), -4.5, 4.5)
    return sample.astype(jnp.bfloat16)


def setup_inputs(seed: int = 0) -> dict:
    seeds = jax.random.split(jax.random.key(seed), 2)
    return {
        "operands": draw_operands(jax.random.fold_in(seeds[1], 71), 0),
    }


def attention_pair(query_rows, out_grad, key_rows, value_rows):
    factor = HEAD ** -0.5
    query_f = query_rows.astype(jnp.float32)
    grad_f = out_grad.astype(jnp.float32)
    key_f = key_rows.astype(jnp.float32)
    value_f = value_rows.astype(jnp.float32)
    scores = jnp.einsum('qhe,khe->hqk', query_f, key_f) * factor
    maximum = jnp.max(scores, axis=-1, keepdims=True)
    exponent = jnp.exp(scores - maximum)
    weights = exponent / jnp.sum(exponent, axis=-1, keepdims=True)
    weights_b = lax.optimization_barrier(weights.astype(jnp.bfloat16)).astype(jnp.float32)
    attended = jnp.einsum('hqk,khe->qhe', weights_b, value_f)
    grad_weights = jnp.einsum('qhe,khe->hqk', grad_f, value_f)
    row_delta = jnp.transpose(jnp.sum(grad_f * attended, axis=-1), (1, 0))[:, :, None]
    grad_scores = weights * (grad_weights - row_delta) * factor
    grad_scores = lax.optimization_barrier(grad_scores.astype(jnp.bfloat16)).astype(jnp.float32)
    query_grad = jnp.einsum('hqk,khe->qhe', grad_scores, key_f)
    key_grad = jnp.einsum('hqk,qhe->khe', grad_scores, query_f)
    value_grad = jnp.einsum('hqk,qhe->khe', weights_b, grad_f)
    return attended, query_grad, key_grad, value_grad


def as_heads(half):
    return half.reshape(ROWS, HEADS, HEAD)


def one_sequence(pair):
    encoder_side = pair[0]
    decoder_side = pair[1]
    key_rows = as_heads(encoder_side[:, :INNER])
    value_rows = as_heads(encoder_side[:, INNER:])
    query_rows = as_heads(decoder_side[:, :INNER])
    out_grad = as_heads(decoder_side[:, INNER:])
    attended, query_grad, key_grad, value_grad = attention_pair(query_rows, out_grad, key_rows, value_rows)
    encoder_out = jnp.concatenate([key_grad.reshape(ROWS, INNER), value_grad.reshape(ROWS, INNER)], axis=-1)
    decoder_out = jnp.concatenate([attended.reshape(ROWS, INNER), query_grad.reshape(ROWS, INNER)], axis=-1)
    return jnp.stack([encoder_out, decoder_out]).astype(jnp.bfloat16)


def reference(operands):
    per_sequence = jnp.moveaxis(operands, 1, 0)
    results = lax.map(one_sequence, per_sequence)
    return jnp.moveaxis(results, 0, 1)
```

```python
import functools

import jax
import jax.numpy as jnp
from jax import lax
from jax.experimental import pallas as pl
from jax.experimental.pallas import tpu as pltpu
from jax.sharding import PartitionSpec as P

HEAD = 256
INNER = 2048
KEPT = INNER // 2
CHUNKS = (1, 1, 1, 1)
FACTOR = HEAD ** (-0.5)


def dot(a, b, dims):
    return lax.dot_general(a, b, (dims, ((), ())), preferred_element_type=jnp.float32)


def head_work(query, out_grad, key, value):
    scores = dot(query, key, ((1,), (1,))) * FACTOR
    grad_weights = dot(out_grad, value, ((1,), (1,)))
    exponent = jnp.exp(scores - jnp.max(scores, axis=-1, keepdims=True))
    weights = exponent / jnp.sum(exponent, axis=-1, keepdims=True)
    weights_b = weights.astype(jnp.bfloat16)
    attended = dot(weights_b, value, ((1,), (0,)))
    value_grad = dot(weights_b, out_grad, ((0,), (0,)))
    row_delta = jnp.sum(out_grad.astype(jnp.float32) * attended, axis=-1, keepdims=True)
    grad_scores = (weights * (grad_weights - row_delta) * FACTOR).astype(jnp.bfloat16)
    query_grad = dot(grad_scores, key, ((1,), (0,)))
    key_grad = dot(grad_scores, query, ((0,), (0,)))
    return tuple(x.astype(jnp.bfloat16) for x in (attended, query_grad, key_grad, value_grad))


def halves(block, chunk, sems, at, width):
    views = [block.at[:, pl.ds(pl.multiple_of(i * INNER + at, HEAD), width)] for i in range(2)]
    return views, [chunk.at[i] for i in range(2)], [sems.at[i] for i in range(2)]


def load(block, chunk, sems, at, width):
    views, parts, s = halves(block, chunk, sems, at, width)
    return [pltpu.make_async_copy(v, p, m) for v, p, m in zip(views, parts, s)]


def store(block, chunk, sems, at, width):
    views, parts, s = halves(block, chunk, sems, at, width)
    return [pltpu.make_async_copy(p, v, m) for v, p, m in zip(views, parts, s)]


def pack_kernel(role_ref, block, *rest):
    *chunks, sems = rest
    at = (1 - role_ref[0]) * KEPT
    copies = []
    for i, chunk in enumerate(chunks):
        copies += load(block, chunk, sems.at[i], at, chunk.shape[-1])
        at = at + chunk.shape[-1]
    for copy in copies:
        copy.start()
    for copy in copies:
        copy.wait()


def work_kernel(first, width, has_out, role_ref, block, received, *rest):
    if has_out:
        rest = rest[1:]
    out, back, own, kept, sems = rest
    role = role_ref[0]
    at = role * KEPT + first
    copies = load(block, own, sems, at, width)
    for copy in copies:
        copy.start()
    for copy in copies:
        copy.wait()

    def run(decoder):
        query_side, key_side = (own, received) if decoder else (received, own)
        front, rear = (kept, back) if decoder else (back, kept)
        for h in range(width // HEAD):
            cols = slice(h * HEAD, (h + 1) * HEAD)
            attended, query_grad, key_grad, value_grad = head_work(
                query_side[0, :, cols], query_side[1, :, cols], key_side[0, :, cols], key_side[1, :, cols]
            )
            front[0, :, cols] = attended
            front[1, :, cols] = query_grad
            rear[0, :, cols] = key_grad
            rear[1, :, cols] = value_grad

    pl.when(role == 1)(lambda: run(True))
    pl.when(role == 0)(lambda: run(False))
    copies = store(out, kept, sems, at, width)
    for copy in copies:
        copy.start()
    for copy in copies:
        copy.wait()


def place_kernel(first, width, role_ref, chunk, _, out, sems):
    at = (1 - role_ref[0]) * KEPT + first
    copies = store(out, chunk, sems, at, width)
    for copy in copies:
        copy.start()
    for copy in copies:
        copy.wait()


SMEM = pl.BlockSpec(memory_space=pltpu.SMEM)
VMEM = pl.BlockSpec(memory_space=pltpu.VMEM)
ANY = pl.BlockSpec(memory_space=pl.ANY)


def chunk_shape(rows, width):
    return jax.ShapeDtypeStruct((2, rows, width), jnp.bfloat16)


def local(operands):
    rows, both = operands.shape[2:]
    block = operands.reshape(rows, both)
    role = lax.axis_index("group").astype(jnp.int32).reshape(1)
    count = lax.axis_size("dp")
    pairs = [(i, (i + count) % (2 * count)) for i in range(2 * count)]
    widths = [n * HEAD for n in CHUNKS]
    firsts = [sum(widths[:i]) for i in range(len(widths))]

    sent = pl.pallas_call(
        pack_kernel,
        out_shape=[chunk_shape(rows, w) for w in widths],
        in_specs=[SMEM, ANY],
        out_specs=[ANY] * len(widths),
        scratch_shapes=[pltpu.SemaphoreType.DMA((len(widths), 2))],
        name="pack",
    )(role, block)
    received = [lax.ppermute(c, ("group", "dp"), pairs) for c in sent]

    out = None
    returned = []
    for first, width, chunk in zip(firsts, widths, received):
        args = [role, block, chunk] + ([out] if out is not None else [])
        out, back = pl.pallas_call(
            functools.partial(work_kernel, first, width, out is not None),
            out_shape=[jax.ShapeDtypeStruct((rows, both), jnp.bfloat16), chunk_shape(rows, width)],
            in_specs=[SMEM, ANY, VMEM] + ([ANY] if out is not None else []),
            out_specs=[ANY, VMEM],
            scratch_shapes=[
                pltpu.VMEM((2, rows, width), jnp.bfloat16),
                pltpu.VMEM((2, rows, width), jnp.bfloat16),
                pltpu.SemaphoreType.DMA((2,)),
            ],
            input_output_aliases={3: 0} if out is not None else {},
            cost_estimate=pl.CostEstimate(
                flops=12 * rows * rows * width, bytes_accessed=16 * rows * width, transcendentals=rows * width
            ),
            name="work",
        )(*args)
        returned.append(lax.ppermute(back, ("group", "dp"), pairs))
    for first, width, chunk in zip(firsts, widths, returned):
        out = pl.pallas_call(
            functools.partial(place_kernel, first, width),
            out_shape=jax.ShapeDtypeStruct((rows, both), jnp.bfloat16),
            in_specs=[SMEM, ANY, ANY],
            out_specs=ANY,
            scratch_shapes=[pltpu.SemaphoreType.DMA((2,))],
            input_output_aliases={2: 0},
            name="place",
        )(role, chunk, out)
    return out.reshape(operands.shape)


def solution(mesh):
    spec = P("group", "dp", None, None)
    return jax.shard_map(local, mesh=mesh, in_specs=(spec,), out_specs=spec, check_vma=False)
```

```python
import functools

import jax
import jax.numpy as jnp
from jax import lax
from jax.experimental import pallas as pl
from jax.experimental.pallas import tpu as pltpu
from jax.sharding import PartitionSpec as P

HEAD = 256
INNER = 2048
KEPT = INNER // 2
CHUNKS = (1, 1, 1, 1)
FACTOR = HEAD ** (-0.5)
VMEM_LIMIT = 12 * 1024 * 1024

SMEM = pl.BlockSpec(memory_space=pltpu.SMEM)
VMEM = pl.BlockSpec(memory_space=pltpu.VMEM)
ANY = pl.BlockSpec(memory_space=pl.ANY)
PARAMS = pltpu.CompilerParams(vmem_limit_bytes=VMEM_LIMIT)


def dot(a, b, dims):
    return lax.dot_general(a, b, (dims, ((), ())), preferred_element_type=jnp.float32)


def head_work(query, out_grad, key, value):
    scores = dot(query, key, ((1,), (1,))) * FACTOR
    grad_weights = dot(out_grad, value, ((1,), (1,)))
    exponent = jnp.exp(scores - jnp.max(scores, axis=-1, keepdims=True))
    weights = exponent / jnp.sum(exponent, axis=-1, keepdims=True)
    weights_b = weights.astype(jnp.bfloat16)
    attended = dot(weights_b, value, ((1,), (0,)))
    value_grad = dot(weights_b, out_grad, ((0,), (0,)))
    row_delta = jnp.sum(out_grad.astype(jnp.float32) * attended, axis=-1, keepdims=True)
    grad_scores = (weights * (grad_weights - row_delta) * FACTOR).astype(jnp.bfloat16)
    query_grad = dot(grad_scores, key, ((1,), (0,)))
    key_grad = dot(grad_scores, query, ((0,), (0,)))
    return tuple(x.astype(jnp.bfloat16) for x in (attended, query_grad, key_grad, value_grad))


def views(block, at, width):
    return [block.at[:, pl.ds(pl.multiple_of(i * INNER + at, HEAD), width)] for i in range(2)]


def run_copies(copies):
    for copy in copies:
        copy.start()
    for copy in copies:
        copy.wait()


def load_kernel(kept, role_ref, block, *rest):
    *chunks, sems = rest
    at = (role_ref[0] if kept else 1 - role_ref[0]) * KEPT
    copies = []
    for i, chunk in enumerate(chunks):
        for j, view in enumerate(views(block, at, chunk.shape[-1])):
            copies.append(pltpu.make_async_copy(view, chunk.at[j], sems.at[i, j]))
        at = at + chunk.shape[-1]
    run_copies(copies)


def work_kernel(width, role_ref, own, received, kept, back):
    role = role_ref[0]

    def run(decoder):
        query_side, key_side = (own, received) if decoder else (received, own)
        front, rear = (kept, back) if decoder else (back, kept)
        for h in range(width // HEAD):
            cols = slice(h * HEAD, (h + 1) * HEAD)
            attended, query_grad, key_grad, value_grad = head_work(
                query_side[0, :, cols], query_side[1, :, cols], key_side[0, :, cols], key_side[1, :, cols]
            )
            front[0, :, cols] = attended
            front[1, :, cols] = query_grad
            rear[0, :, cols] = key_grad
            rear[1, :, cols] = value_grad

    pl.when(role == 1)(lambda: run(True))
    pl.when(role == 0)(lambda: run(False))


def place_kernel(kept, firsts, aliased, role_ref, *rest):
    *chunks, out, sems = rest
    if aliased:
        chunks = chunks[:-1]
    at = (role_ref[0] if kept else 1 - role_ref[0]) * KEPT
    copies = []
    for i, (first, chunk) in enumerate(zip(firsts, chunks)):
        for j, view in enumerate(views(out, at + first, chunk.shape[-1])):
            copies.append(pltpu.make_async_copy(chunk.at[j], view, sems.at[i, j]))
    run_copies(copies)


def chunk_shape(rows, width):
    return jax.ShapeDtypeStruct((2, rows, width), jnp.bfloat16)


def cost(moved, flops=0, exps=0):
    return pl.CostEstimate(flops=flops, bytes_accessed=moved, transcendentals=exps)


def local(operands):
    rows, both = operands.shape[2:]
    block = operands.reshape(rows, both)
    role = lax.axis_index("group").astype(jnp.int32).reshape(1)
    count = lax.axis_size("dp")
    pairs = [(i, (i + count) % (2 * count)) for i in range(2 * count)]
    widths = [n * HEAD for n in CHUNKS]
    firsts = [sum(widths[:i]) for i in range(len(widths))]
    n = len(widths)

    def load(kept):
        return pl.pallas_call(
            functools.partial(load_kernel, kept),
            out_shape=[chunk_shape(rows, w) for w in widths],
            in_specs=[SMEM, ANY],
            out_specs=[VMEM] * n,
            scratch_shapes=[pltpu.SemaphoreType.DMA((n, 2))],
            compiler_params=PARAMS,
            cost_estimate=cost(rows * both),
            name="keep" if kept else "pack",
        )(role, block)

    def work(width, own, received):
        return pl.pallas_call(
            functools.partial(work_kernel, width),
            out_shape=[chunk_shape(rows, width)] * 2,
            in_specs=[SMEM, VMEM, VMEM],
            out_specs=[VMEM, VMEM],
            compiler_params=PARAMS,
            cost_estimate=cost(0, flops=12 * rows * rows * width, exps=rows * width),
            name="work",
        )(role, own, received)

    def place(kept, at, chunks, out=None):
        extra = [] if out is None else [out]
        return pl.pallas_call(
            functools.partial(place_kernel, kept, at, bool(extra)),
            out_shape=jax.ShapeDtypeStruct((rows, both), jnp.bfloat16),
            in_specs=[SMEM] + [VMEM] * len(chunks) + [ANY] * len(extra),
            out_specs=ANY,
            scratch_shapes=[pltpu.SemaphoreType.DMA((len(chunks), 2))],
            input_output_aliases={1 + len(chunks): 0} if extra else {},
            compiler_params=PARAMS,
            cost_estimate=cost(0),
            name="place",
        )(role, *chunks, *extra)

    sent = load(False)
    received = [lax.ppermute(c, ("group", "dp"), pairs) for c in sent]
    own = load(True)
    done, returned = [], []
    for i in range(n):
        kept, back = work(widths[i], own[i], received[i])
        done.append(kept)
        returned.append(lax.ppermute(back, ("group", "dp"), pairs))
    out = place(True, firsts, done)
    for i in range(n):
        out = place(False, [firsts[i]], [returned[i]], out)
    return out.reshape(operands.shape)


def solution(mesh):
    spec = P("group", "dp", None, None)
    return jax.shard_map(local, mesh=mesh, in_specs=(spec,), out_specs=spec, check_vma=False)
```

```python
import functools

import jax
import jax.numpy as jnp
from jax import lax
from jax.experimental import pallas as pl
from jax.experimental.pallas import tpu as pltpu
from jax.sharding import PartitionSpec as P

HEAD = 256
INNER = 2048
KEPT = INNER // 2
CHUNKS = (1, 1, 1, 1)
EARLY = 2
FACTOR = HEAD ** (-0.5)
VMEM_LIMIT = 12 * 1024 * 1024

VMEM = pl.BlockSpec(memory_space=pltpu.VMEM)
ANY = pl.BlockSpec(memory_space=pl.ANY)
HBM = pl.BlockSpec(memory_space=pltpu.HBM)
PARAMS = pltpu.CompilerParams(vmem_limit_bytes=VMEM_LIMIT)


def dot(a, b, dims):
    return lax.dot_general(a, b, (dims, ((), ())), preferred_element_type=jnp.float32)


def head_work(query, out_grad, key, value):
    scores = dot(query, key, ((1,), (1,))) * FACTOR
    grad_weights = dot(out_grad, value, ((1,), (1,)))
    exponent = jnp.exp(scores - jnp.max(scores, axis=-1, keepdims=True))
    weights = exponent / jnp.sum(exponent, axis=-1, keepdims=True)
    weights_b = weights.astype(jnp.bfloat16)
    attended = dot(weights_b, value, ((1,), (0,)))
    value_grad = dot(weights_b, out_grad, ((0,), (0,)))
    row_delta = jnp.sum(out_grad.astype(jnp.float32) * attended, axis=-1, keepdims=True)
    grad_scores = (weights * (grad_weights - row_delta) * FACTOR).astype(jnp.bfloat16)
    query_grad = dot(grad_scores, key, ((1,), (0,)))
    key_grad = dot(grad_scores, query, ((0,), (0,)))
    return tuple(x.astype(jnp.bfloat16) for x in (attended, query_grad, key_grad, value_grad))


def views(block, at, width):
    return [block.at[:, pl.ds(pl.multiple_of(i * INNER + at, HEAD), width)] for i in range(2)]


def side(kept):
    role = lax.axis_index("group")
    return role if kept else 1 - role


def run_copies(copies):
    for copy in copies:
        copy.start()
    for copy in copies:
        copy.wait()


def load_kernel(parts, block, *rest):
    *chunks, sems = rest
    copies = []
    for i, ((kept, first), chunk) in enumerate(zip(parts, chunks)):
        at = side(kept) * KEPT + first
        for j, view in enumerate(views(block, at, chunk.shape[-1])):
            copies.append(pltpu.make_async_copy(view, chunk.at[j], sems.at[i, j]))
    run_copies(copies)


def work_kernel(width, own, received, kept, back):
    role = lax.axis_index("group")

    def run(decoder):
        query_side, key_side = (own, received) if decoder else (received, own)
        front, rear = (kept, back) if decoder else (back, kept)
        for h in range(width // HEAD):
            cols = slice(h * HEAD, (h + 1) * HEAD)
            attended, query_grad, key_grad, value_grad = head_work(
                query_side[0, :, cols], query_side[1, :, cols], key_side[0, :, cols], key_side[1, :, cols]
            )
            front[0, :, cols] = attended
            front[1, :, cols] = query_grad
            rear[0, :, cols] = key_grad
            rear[1, :, cols] = value_grad

    pl.when(role == 1)(lambda: run(True))
    pl.when(role == 0)(lambda: run(False))


def place_kernel(kept, firsts, aliased, *rest):
    *chunks, out, sems = rest
    if aliased:
        chunks = chunks[:-1]
    at = side(kept) * KEPT
    copies = []
    for i, (first, chunk) in enumerate(zip(firsts, chunks)):
        for j, view in enumerate(views(out, at + first, chunk.shape[-1])):
            copies.append(pltpu.make_async_copy(chunk.at[j], view, sems.at[i, j]))
    run_copies(copies)


def chunk_shape(rows, width):
    return jax.ShapeDtypeStruct((2, rows, width), jnp.bfloat16)


def cost(moved, flops=0, exps=0):
    return pl.CostEstimate(flops=flops, bytes_accessed=moved, transcendentals=exps)


def local(operands):
    rows, both = operands.shape[2:]
    count = lax.axis_size("dp")
    pairs = [(i, (i + count) % (2 * count)) for i in range(2 * count)]
    widths = [n * HEAD for n in CHUNKS]
    firsts = [sum(widths[:i]) for i in range(len(widths))]
    n = len(widths)

    def load(parts, block):
        return pl.pallas_call(
            functools.partial(load_kernel, [(kept, firsts[i]) for kept, i in parts]),
            out_shape=[pltpu.VMEM((2, rows, widths[i]), jnp.bfloat16) for _, i in parts],
            in_specs=[HBM],
            out_specs=[VMEM] * len(parts),
            scratch_shapes=[pltpu.SemaphoreType.DMA((len(parts), 2))],
            compiler_params=PARAMS,
            cost_estimate=cost(0),
            name="load",
        )(block)

    def work(width, own, received):
        return pl.pallas_call(
            functools.partial(work_kernel, width),
            out_shape=[chunk_shape(rows, width)] * 2,
            in_specs=[VMEM, VMEM],
            out_specs=[VMEM, VMEM],
            compiler_params=PARAMS,
            cost_estimate=cost(0, flops=12 * rows * rows * width, exps=rows * width),
            name="work",
        )(own, received)

    def place(kept, at, chunks, out=None):
        extra = [] if out is None else [out]
        return pl.pallas_call(
            functools.partial(place_kernel, kept, at, bool(extra)),
            out_shape=jax.ShapeDtypeStruct((rows, both), jnp.bfloat16),
            in_specs=[VMEM] * len(chunks) + [ANY] * len(extra),
            out_specs=ANY,
            scratch_shapes=[pltpu.SemaphoreType.DMA((len(chunks), 2))],
            input_output_aliases={len(chunks): 0} if extra else {},
            compiler_params=PARAMS,
            cost_estimate=cost(0),
            name="place",
        )(*chunks, *extra)

    block = pltpu.with_memory_space_constraint(operands.reshape(rows, both), pltpu.HBM)
    sent = load([(False, i) for i in range(EARLY)], block)
    rest = load([(False, i) for i in range(EARLY, n)] + [(True, i) for i in range(n)], block)
    sent, own = sent + rest[: n - EARLY], rest[n - EARLY :]
    received = [lax.ppermute(c, ("group", "dp"), pairs) for c in sent]
    done, returned = [], []
    for i in range(n):
        kept, back = work(widths[i], own[i], received[i])
        done.append(kept)
        returned.append(lax.ppermute(back, ("group", "dp"), pairs))
    out = place(True, firsts, done)
    for i in range(n):
        out = place(False, [firsts[i]], [returned[i]], out)
    return out.reshape(operands.shape)


def solution(mesh):
    spec = P("group", "dp", None, None)
    return jax.shard_map(local, mesh=mesh, in_specs=(spec,), out_specs=spec, check_vma=False)
```

```python
import functools

import jax
import jax.numpy as jnp
from jax import lax
from jax.experimental import pallas as pl
from jax.experimental.pallas import tpu as pltpu
from jax.sharding import PartitionSpec as P

HEAD = 256
INNER = 2048
KEPT = INNER // 2
CHUNKS = (2, 1, 1)
EARLY = 1
FACTOR = HEAD ** (-0.5)
VMEM_LIMIT = 12 * 1024 * 1024

VMEM = pl.BlockSpec(memory_space=pltpu.VMEM)
ANY = pl.BlockSpec(memory_space=pl.ANY)
HBM = pl.BlockSpec(memory_space=pltpu.HBM)
PARAMS = pltpu.CompilerParams(vmem_limit_bytes=VMEM_LIMIT)


def dot(a, b, dims):
    return lax.dot_general(a, b, (dims, ((), ())), preferred_element_type=jnp.float32)


def head_work(query, out_grad, key, value):
    scores = dot(query, key, ((1,), (1,))) * FACTOR
    grad_weights = dot(out_grad, value, ((1,), (1,)))
    exponent = jnp.exp(scores - jnp.max(scores, axis=-1, keepdims=True))
    weights = exponent / jnp.sum(exponent, axis=-1, keepdims=True)
    weights_b = weights.astype(jnp.bfloat16)
    attended = dot(weights_b, value, ((1,), (0,)))
    value_grad = dot(weights_b, out_grad, ((0,), (0,)))
    row_delta = jnp.sum(out_grad.astype(jnp.float32) * attended, axis=-1, keepdims=True)
    grad_scores = (weights * (grad_weights - row_delta) * FACTOR).astype(jnp.bfloat16)
    query_grad = dot(grad_scores, key, ((1,), (0,)))
    key_grad = dot(grad_scores, query, ((0,), (0,)))
    return tuple(x.astype(jnp.bfloat16) for x in (attended, query_grad, key_grad, value_grad))


def views(block, at, width):
    return [block.at[:, pl.ds(pl.multiple_of(i * INNER + at, HEAD), width)] for i in range(2)]


def side(kept):
    role = lax.axis_index("group")
    return role if kept else 1 - role


def run_copies(copies):
    for copy in copies:
        copy.start()
    for copy in copies:
        copy.wait()


def load_kernel(parts, block, *rest):
    *chunks, sems = rest
    copies = []
    for i, ((kept, first), chunk) in enumerate(zip(parts, chunks)):
        at = side(kept) * KEPT + first
        for j, view in enumerate(views(block, at, chunk.shape[-1])):
            copies.append(pltpu.make_async_copy(view, chunk.at[j], sems.at[i, j]))
    run_copies(copies)


def work_kernel(width, own, received, kept, back):
    role = lax.axis_index("group")

    def run(decoder):
        query_side, key_side = (own, received) if decoder else (received, own)
        front, rear = (kept, back) if decoder else (back, kept)
        for h in range(width // HEAD):
            cols = slice(h * HEAD, (h + 1) * HEAD)
            attended, query_grad, key_grad, value_grad = head_work(
                query_side[0, :, cols], query_side[1, :, cols], key_side[0, :, cols], key_side[1, :, cols]
            )
            front[0, :, cols] = attended
            front[1, :, cols] = query_grad
            rear[0, :, cols] = key_grad
            rear[1, :, cols] = value_grad

    pl.when(role == 1)(lambda: run(True))
    pl.when(role == 0)(lambda: run(False))


def place_kernel(kept, firsts, aliased, *rest):
    *chunks, out, sems = rest
    if aliased:
        chunks = chunks[:-1]
    at = side(kept) * KEPT
    copies = []
    for i, (first, chunk) in enumerate(zip(firsts, chunks)):
        for j, view in enumerate(views(out, at + first, chunk.shape[-1])):
            copies.append(pltpu.make_async_copy(chunk.at[j], view, sems.at[i, j]))
    run_copies(copies)


def chunk_shape(rows, width):
    return jax.ShapeDtypeStruct((2, rows, width), jnp.bfloat16)


def cost(moved, flops=0, exps=0):
    return pl.CostEstimate(flops=flops, bytes_accessed=moved, transcendentals=exps)


def local(operands):
    rows, both = operands.shape[2:]
    count = lax.axis_size("dp")
    pairs = [(i, (i + count) % (2 * count)) for i in range(2 * count)]
    widths = [n * HEAD for n in CHUNKS]
    firsts = [sum(widths[:i]) for i in range(len(widths))]
    n = len(widths)

    def load(parts, block):
        return pl.pallas_call(
            functools.partial(load_kernel, [(kept, firsts[i]) for kept, i in parts]),
            out_shape=[pltpu.VMEM((2, rows, widths[i]), jnp.bfloat16) for _, i in parts],
            in_specs=[HBM],
            out_specs=[VMEM] * len(parts),
            scratch_shapes=[pltpu.SemaphoreType.DMA((len(parts), 2))],
            compiler_params=PARAMS,
            cost_estimate=cost(0),
            name="load",
        )(block)

    def work(width, own, received):
        return pl.pallas_call(
            functools.partial(work_kernel, width),
            out_shape=[chunk_shape(rows, width)] * 2,
            in_specs=[VMEM, VMEM],
            out_specs=[VMEM, VMEM],
            compiler_params=PARAMS,
            cost_estimate=cost(0, flops=12 * rows * rows * width, exps=rows * width),
            name="work",
        )(own, received)

    def place(kept, at, chunks, out=None):
        extra = [] if out is None else [out]
        return pl.pallas_call(
            functools.partial(place_kernel, kept, at, bool(extra)),
            out_shape=jax.ShapeDtypeStruct((rows, both), jnp.bfloat16),
            in_specs=[VMEM] * len(chunks) + [ANY] * len(extra),
            out_specs=ANY,
            scratch_shapes=[pltpu.SemaphoreType.DMA((len(chunks), 2))],
            input_output_aliases={len(chunks): 0} if extra else {},
            compiler_params=PARAMS,
            cost_estimate=cost(0),
            name="place",
        )(*chunks, *extra)

    block = pltpu.with_memory_space_constraint(operands.reshape(rows, both), pltpu.HBM)
    sent = load([(False, i) for i in range(EARLY)], block)
    rest = load([(False, i) for i in range(EARLY, n)] + [(True, i) for i in range(n)], block)
    sent, own = sent + rest[: n - EARLY], rest[n - EARLY :]
    received = [lax.ppermute(c, ("group", "dp"), pairs) for c in sent]
    done, returned = [], []
    for i in range(n):
        kept, back = work(widths[i], own[i], received[i])
        done.append(kept)
        returned.append(lax.ppermute(back, ("group", "dp"), pairs))
    out = place(True, firsts, done)
    for i in range(n):
        out = place(False, [firsts[i]], [returned[i]], out)
    return out.reshape(operands.shape)


def solution(mesh):
    spec = P("group", "dp", None, None)
    return jax.shard_map(local, mesh=mesh, in_specs=(spec,), out_specs=spec, check_vma=False)
```

```python
import functools

import jax
import jax.numpy as jnp
from jax import lax
from jax.experimental import pallas as pl
from jax.experimental.pallas import tpu as pltpu
from jax.sharding import PartitionSpec as P

HEAD = 256
HEADS = 8
INNER = HEAD * HEADS
KEPT = INNER // 2
CHUNKS = (1, 1, 1, 1)
LOAD_GROUPS = 3
FACTOR = HEAD ** (-0.5)
PARAMS = pltpu.CompilerParams(vmem_limit_bytes=12 * 1024 * 1024)

VMEM = pl.BlockSpec(memory_space=pltpu.VMEM)
ANY = pl.BlockSpec(memory_space=pl.ANY)
HBM = pl.BlockSpec(memory_space=pltpu.HBM)


def dot(a, b, dims):
    return lax.dot_general(a, b, (dims, ((), ())), preferred_element_type=jnp.float32)


def softmax(scores, axis):
    exponent = jnp.exp(scores - jnp.max(scores, axis=axis, keepdims=True))
    return exponent / jnp.sum(exponent, axis=axis, keepdims=True)


def decoder_half(query, out_grad, key, value):
    weights = softmax(dot(query, key, ((1,), (1,))) * FACTOR, -1)
    grad_weights = dot(out_grad, value, ((1,), (1,)))
    weights_b = weights.astype(jnp.bfloat16)
    attended = dot(weights_b, value, ((1,), (0,)))
    row_delta = jnp.sum(out_grad.astype(jnp.float32) * attended, axis=-1, keepdims=True)
    grad_scores = (weights * (grad_weights - row_delta) * FACTOR).astype(jnp.bfloat16)
    query_grad = dot(grad_scores, key, ((1,), (0,)))
    return attended.astype(jnp.bfloat16), query_grad.astype(jnp.bfloat16), weights_b, grad_scores


def encoder_half(query, out_grad, key, value):
    weights = softmax(dot(key, query, ((1,), (1,))) * FACTOR, 0)
    grad_weights = dot(value, out_grad, ((1,), (1,)))
    weights_b = weights.astype(jnp.bfloat16)
    row_delta = jnp.sum(weights_b.astype(jnp.float32) * grad_weights, axis=0, keepdims=True)
    grad_scores = (weights * (grad_weights - row_delta) * FACTOR).astype(jnp.bfloat16)
    key_grad = dot(grad_scores, query, ((1,), (0,)))
    value_grad = dot(weights_b, out_grad, ((1,), (0,)))
    return key_grad.astype(jnp.bfloat16), value_grad.astype(jnp.bfloat16)


def head_work(query, out_grad, key, value):
    attended, query_grad, weights_b, grad_scores = decoder_half(query, out_grad, key, value)
    key_grad = dot(grad_scores, query, ((0,), (0,))).astype(jnp.bfloat16)
    value_grad = dot(weights_b, out_grad, ((0,), (0,))).astype(jnp.bfloat16)
    return attended, query_grad, key_grad, value_grad


def on_decoder():
    return lax.axis_index("group") == 1


def in_split_plan():
    return lax.rem(lax.axis_index("dp"), 2) == 0


def side(kept):
    role = lax.axis_index("group")
    return role if kept else 1 - role


def views(block, at, width):
    return [block.at[:, pl.ds(pl.multiple_of(i * INNER + at, HEAD), width)] for i in range(2)]


def run_copies(copies):
    for copy in copies:
        copy.start()
    for copy in copies:
        copy.wait()


def load_kernel(parts, groups, block, *rest):
    *chunks, whole, sems = rest

    def split():
        copies = []
        for i, ((kept, first), chunk) in enumerate(zip(parts, chunks)):
            for j, view in enumerate(views(block, side(kept) * KEPT + first, chunk.shape[-1])):
                copies.append(pltpu.make_async_copy(view, chunk.at[j], sems.at[i, j]))
        size = -(-len(copies) // groups)
        for i in range(0, len(copies), size):
            run_copies(copies[i : i + size])

    def all_of_it():
        run_copies([pltpu.make_async_copy(block, whole, sems.at[0, 0])])

    pl.when(in_split_plan())(split)
    pl.when(jnp.logical_not(in_split_plan()))(all_of_it)


def work_kernel(width, own, received, kept, back):
    def run(decoder):
        query_side, key_side = (own, received) if decoder else (received, own)
        front, rear = (kept, back) if decoder else (back, kept)
        for h in range(width // HEAD):
            cols = slice(h * HEAD, (h + 1) * HEAD)
            attended, query_grad, key_grad, value_grad = head_work(
                query_side[0, :, cols], query_side[1, :, cols], key_side[0, :, cols], key_side[1, :, cols]
            )
            front[0, :, cols] = attended
            front[1, :, cols] = query_grad
            rear[0, :, cols] = key_grad
            rear[1, :, cols] = value_grad

    split = in_split_plan()
    pl.when(jnp.logical_and(split, on_decoder()))(lambda: run(True))
    pl.when(jnp.logical_and(split, jnp.logical_not(on_decoder())))(lambda: run(False))


def whole_kernel(own, received, _, out, stage, sems):
    def run(decoder):
        query_side, key_side = (own, received) if decoder else (received, own)
        copies = []
        for h in range(HEADS):
            cols = [slice(i * INNER + h * HEAD, i * INNER + (h + 1) * HEAD) for i in range(2)]
            operands = [ref[:, c] for ref in (query_side, key_side) for c in cols]
            results = (decoder_half if decoder else encoder_half)(*operands)[:2]
            for i, result in enumerate(results):
                stage[h, i] = result
                copies.append(pltpu.make_async_copy(stage.at[h, i], out.at[:, cols[i]], sems.at[h, i]))
                copies[-1].start()
        for copy in copies:
            copy.wait()

    whole = jnp.logical_not(in_split_plan())
    pl.when(jnp.logical_and(whole, on_decoder()))(lambda: run(True))
    pl.when(jnp.logical_and(whole, jnp.logical_not(on_decoder())))(lambda: run(False))


def place_kernel(kept, firsts, aliased, *rest):
    *chunks, out, sems = rest
    if aliased:
        chunks = chunks[:-1]

    def run():
        copies = []
        for i, (first, chunk) in enumerate(zip(firsts, chunks)):
            for j, view in enumerate(views(out, side(kept) * KEPT + first, chunk.shape[-1])):
                copies.append(pltpu.make_async_copy(chunk.at[j], view, sems.at[i, j]))
        run_copies(copies)

    pl.when(in_split_plan())(run)


def cost(moved, flops=0, exps=0):
    return pl.CostEstimate(flops=flops, bytes_accessed=moved, transcendentals=exps)


def local(operands):
    rows, both = operands.shape[2:]
    count = lax.axis_size("dp")
    swaps = [(i, (i + count) % (2 * count)) for i in range(2 * count)]
    split_swaps = [p for p in swaps if p[0] % 2 == 0]
    whole_swaps = [p for p in swaps if p[0] % 2 == 1]
    widths = [n * HEAD for n in CHUNKS]
    firsts = [sum(widths[:i]) for i in range(len(widths))]
    n = len(widths)

    def load(block, parts):
        return pl.pallas_call(
            functools.partial(load_kernel, [(kept, firsts[i]) for kept, i in parts], LOAD_GROUPS),
            out_shape=[pltpu.VMEM((2, rows, widths[i]), jnp.bfloat16) for _, i in parts]
            + [pltpu.VMEM((rows, both), jnp.bfloat16)],
            in_specs=[HBM],
            out_specs=[VMEM] * (len(parts) + 1),
            scratch_shapes=[pltpu.SemaphoreType.DMA((len(parts), 2))],
            compiler_params=PARAMS,
            cost_estimate=cost(0),
            name="load",
        )(block)

    def work(width, own, received):
        return pl.pallas_call(
            functools.partial(work_kernel, width),
            out_shape=[jax.ShapeDtypeStruct((2, rows, width), jnp.bfloat16)] * 2,
            in_specs=[VMEM, VMEM],
            out_specs=[VMEM, VMEM],
            compiler_params=PARAMS,
            cost_estimate=cost(0, flops=12 * rows * rows * width, exps=rows * width),
            name="work",
        )(own, received)

    def place(kept, at, chunks, out=None):
        extra = [] if out is None else [out]
        return pl.pallas_call(
            functools.partial(place_kernel, kept, at, bool(extra)),
            out_shape=jax.ShapeDtypeStruct((rows, both), jnp.bfloat16),
            in_specs=[VMEM] * len(chunks) + [ANY] * len(extra),
            out_specs=ANY,
            scratch_shapes=[pltpu.SemaphoreType.DMA((len(chunks), 2))],
            input_output_aliases={len(chunks): 0} if extra else {},
            compiler_params=PARAMS,
            cost_estimate=cost(0),
            name="place",
        )(*chunks, *extra)

    def whole(own, received, out):
        return pl.pallas_call(
            whole_kernel,
            out_shape=jax.ShapeDtypeStruct((rows, both), jnp.bfloat16),
            in_specs=[VMEM, VMEM, ANY],
            out_specs=ANY,
            scratch_shapes=[
                pltpu.VMEM((HEADS, 2, rows, HEAD), jnp.bfloat16),
                pltpu.SemaphoreType.DMA((HEADS, 2)),
            ],
            input_output_aliases={2: 0},
            compiler_params=PARAMS,
            cost_estimate=cost(0),
            name="whole",
        )(own, received, out)

    whole_received = lax.ppermute(operands, ("group", "dp"), whole_swaps)
    block = pltpu.with_memory_space_constraint(operands.reshape(rows, both), pltpu.HBM)
    *chunks, own_block = load(block, [(True, i) for i in range(n)] + [(False, i) for i in range(n)])
    own, sent = chunks[:n], chunks[n:]
    received = [lax.ppermute(c, ("group", "dp"), split_swaps) for c in sent]
    done, returned = [], []
    for i in range(n):
        kept, back = work(widths[i], own[i], received[i])
        done.append(kept)
        returned.append(lax.ppermute(back, ("group", "dp"), split_swaps))
    out = place(True, firsts, done)
    for i in range(n):
        if i == n - 1:
            out = whole(own_block, whole_received.reshape(rows, both), out)
        out = place(False, [firsts[i]], [returned[i]], out)
    return out.reshape(operands.shape)


def solution(mesh):
    spec = P("group", "dp", None, None)
    return jax.shard_map(local, mesh=mesh, in_specs=(spec,), out_specs=spec, check_vma=False)
```

```python
import functools

import jax
import jax.numpy as jnp
from jax import lax
from jax.experimental import pallas as pl
from jax.experimental.pallas import tpu as pltpu
from jax.sharding import PartitionSpec as P

HEAD = 256
HEADS = 8
INNER = HEAD * HEADS
KEPT = INNER // 2
CHUNKS = (1, 1, 1, 1)
TOGETHER = 4
FACTOR = HEAD ** (-0.5)
PARAMS = pltpu.CompilerParams(vmem_limit_bytes=12 * 1024 * 1024)

VMEM = pl.BlockSpec(memory_space=pltpu.VMEM)
ANY = pl.BlockSpec(memory_space=pl.ANY)
HBM = pl.BlockSpec(memory_space=pltpu.HBM)


def dot(a, b, dims):
    return lax.dot_general(a, b, (dims, ((), ())), preferred_element_type=jnp.float32)


def softmax(scores, axis):
    exponent = jnp.exp(scores - jnp.max(scores, axis=axis, keepdims=True))
    return exponent / jnp.sum(exponent, axis=axis, keepdims=True)


def decoder_half(query, out_grad, key, value):
    scores = dot(query, key, ((1,), (1,))) * FACTOR
    grad_weights = dot(out_grad, value, ((1,), (1,)))
    yield
    weights = softmax(scores, -1)
    weights_b = weights.astype(jnp.bfloat16)
    yield
    attended = dot(weights_b, value, ((1,), (0,)))
    yield
    row_delta = jnp.sum(out_grad.astype(jnp.float32) * attended, axis=-1, keepdims=True)
    grad_scores = (weights * (grad_weights - row_delta) * FACTOR).astype(jnp.bfloat16)
    yield
    query_grad = dot(grad_scores, key, ((1,), (0,)))
    return attended.astype(jnp.bfloat16), query_grad.astype(jnp.bfloat16), weights_b, grad_scores


def encoder_half(query, out_grad, key, value):
    scores = dot(key, query, ((1,), (1,))) * FACTOR
    grad_weights = dot(value, out_grad, ((1,), (1,)))
    yield
    weights = softmax(scores, 0)
    weights_b = weights.astype(jnp.bfloat16)
    yield
    value_grad = dot(weights_b, out_grad, ((1,), (0,)))
    row_delta = jnp.sum(weights_b.astype(jnp.float32) * grad_weights, axis=0, keepdims=True)
    grad_scores = (weights * (grad_weights - row_delta) * FACTOR).astype(jnp.bfloat16)
    yield
    key_grad = dot(grad_scores, query, ((1,), (0,)))
    return key_grad.astype(jnp.bfloat16), value_grad.astype(jnp.bfloat16)


def head_work(query, out_grad, key, value):
    attended, query_grad, weights_b, grad_scores = yield from decoder_half(query, out_grad, key, value)
    yield
    key_grad = dot(grad_scores, query, ((0,), (0,))).astype(jnp.bfloat16)
    value_grad = dot(weights_b, out_grad, ((0,), (0,))).astype(jnp.bfloat16)
    return attended, query_grad, key_grad, value_grad


def side_by_side(heads):
    results = [None] * len(heads)
    left = list(range(len(heads)))
    while left:
        for i in list(left):
            try:
                next(heads[i])
            except StopIteration as end:
                results[i] = end.value
                left.remove(i)
    return results


def on_decoder():
    return lax.axis_index("group") == 1


def in_split_plan():
    return lax.rem(lax.axis_index("dp"), 2) == 0


def side(kept):
    role = lax.axis_index("group")
    return role if kept else 1 - role


def views(block, at, width):
    return [block.at[:, pl.ds(pl.multiple_of(i * INNER + at, HEAD), width)] for i in range(2)]


def run_copies(copies):
    for copy in copies:
        copy.start()
    for copy in copies:
        copy.wait()


def load_kernel(parts, block, *rest):
    *chunks, whole, sems = rest

    def split():
        copies = []
        for i, ((kept, first), chunk) in enumerate(zip(parts, chunks)):
            for j, view in enumerate(views(block, side(kept) * KEPT + first, chunk.shape[-1])):
                copies.append(pltpu.make_async_copy(view, chunk.at[j], sems.at[i, j]))
        run_copies(copies)

    def all_of_it():
        run_copies([pltpu.make_async_copy(block, whole, sems.at[0, 0])])

    pl.when(in_split_plan())(split)
    pl.when(jnp.logical_not(in_split_plan()))(all_of_it)


def work_kernel(width, own, received, kept, back):
    def run(decoder):
        query_side, key_side = (own, received) if decoder else (received, own)
        front, rear = (kept, back) if decoder else (back, kept)
        cols = [slice(h * HEAD, (h + 1) * HEAD) for h in range(width // HEAD)]
        heads = [
            head_work(query_side[0, :, c], query_side[1, :, c], key_side[0, :, c], key_side[1, :, c]) for c in cols
        ]
        for c, (attended, query_grad, key_grad, value_grad) in zip(cols, side_by_side(heads)):
            front[0, :, c] = attended
            front[1, :, c] = query_grad
            rear[0, :, c] = key_grad
            rear[1, :, c] = value_grad

    split = in_split_plan()
    pl.when(jnp.logical_and(split, on_decoder()))(lambda: run(True))
    pl.when(jnp.logical_and(split, jnp.logical_not(on_decoder())))(lambda: run(False))


def whole_kernel(own, received, _, out, stage, sems):
    def run(decoder):
        query_side, key_side = (own, received) if decoder else (received, own)
        copies = []
        for start in range(0, HEADS, TOGETHER):
            heads = range(start, start + TOGETHER)
            cols = {h: [slice(i * INNER + h * HEAD, i * INNER + (h + 1) * HEAD) for i in range(2)] for h in heads}
            work = decoder_half if decoder else encoder_half
            results = side_by_side([work(*[ref[:, c] for ref in (query_side, key_side) for c in cols[h]]) for h in heads])
            for h, result in zip(heads, results):
                for i in range(2):
                    stage[h, i] = result[i]
                    copies.append(pltpu.make_async_copy(stage.at[h, i], out.at[:, cols[h][i]], sems.at[h, i]))
                    copies[-1].start()
        for copy in copies:
            copy.wait()

    whole = jnp.logical_not(in_split_plan())
    pl.when(jnp.logical_and(whole, on_decoder()))(lambda: run(True))
    pl.when(jnp.logical_and(whole, jnp.logical_not(on_decoder())))(lambda: run(False))


def place_kernel(kept, firsts, aliased, *rest):
    *chunks, out, sems = rest
    if aliased:
        chunks = chunks[:-1]

    def run():
        copies = []
        for i, (first, chunk) in enumerate(zip(firsts, chunks)):
            for j, view in enumerate(views(out, side(kept) * KEPT + first, chunk.shape[-1])):
                copies.append(pltpu.make_async_copy(chunk.at[j], view, sems.at[i, j]))
        run_copies(copies)

    pl.when(in_split_plan())(run)


def cost(moved, flops=0, exps=0):
    return pl.CostEstimate(flops=flops, bytes_accessed=moved, transcendentals=exps)


def local(operands):
    rows, both = operands.shape[2:]
    count = lax.axis_size("dp")
    swaps = [(i, (i + count) % (2 * count)) for i in range(2 * count)]
    split_swaps = [p for p in swaps if p[0] % 2 == 0]
    whole_swaps = [p for p in swaps if p[0] % 2 == 1]
    widths = [n * HEAD for n in CHUNKS]
    firsts = [sum(widths[:i]) for i in range(len(widths))]
    n = len(widths)

    def load(block, parts):
        return pl.pallas_call(
            functools.partial(load_kernel, [(kept, firsts[i]) for kept, i in parts]),
            out_shape=[pltpu.VMEM((2, rows, widths[i]), jnp.bfloat16) for _, i in parts]
            + [pltpu.VMEM((rows, both), jnp.bfloat16)],
            in_specs=[HBM],
            out_specs=[VMEM] * (len(parts) + 1),
            scratch_shapes=[pltpu.SemaphoreType.DMA((len(parts), 2))],
            compiler_params=PARAMS,
            cost_estimate=cost(0),
            name="load",
        )(block)

    def work(width, own, received):
        return pl.pallas_call(
            functools.partial(work_kernel, width),
            out_shape=[jax.ShapeDtypeStruct((2, rows, width), jnp.bfloat16)] * 2,
            in_specs=[VMEM, VMEM],
            out_specs=[VMEM, VMEM],
            compiler_params=PARAMS,
            cost_estimate=cost(0, flops=12 * rows * rows * width, exps=rows * width),
            name="work",
        )(own, received)

    def place(kept, at, chunks, out=None):
        extra = [] if out is None else [out]
        return pl.pallas_call(
            functools.partial(place_kernel, kept, at, bool(extra)),
            out_shape=jax.ShapeDtypeStruct((rows, both), jnp.bfloat16),
            in_specs=[VMEM] * len(chunks) + [ANY] * len(extra),
            out_specs=ANY,
            scratch_shapes=[pltpu.SemaphoreType.DMA((len(chunks), 2))],
            input_output_aliases={len(chunks): 0} if extra else {},
            compiler_params=PARAMS,
            cost_estimate=cost(0),
            name="place",
        )(*chunks, *extra)

    def whole(own, received, out):
        return pl.pallas_call(
            whole_kernel,
            out_shape=jax.ShapeDtypeStruct((rows, both), jnp.bfloat16),
            in_specs=[VMEM, VMEM, ANY],
            out_specs=ANY,
            scratch_shapes=[
                pltpu.VMEM((HEADS, 2, rows, HEAD), jnp.bfloat16),
                pltpu.SemaphoreType.DMA((HEADS, 2)),
            ],
            input_output_aliases={2: 0},
            compiler_params=PARAMS,
            cost_estimate=cost(0),
            name="whole",
        )(own, received, out)

    whole_received = lax.ppermute(operands, ("group", "dp"), whole_swaps)
    block = pltpu.with_memory_space_constraint(operands.reshape(rows, both), pltpu.HBM)
    *chunks, own_block = load(block, [(True, i) for i in range(n)] + [(False, i) for i in range(n)])
    own, sent = chunks[:n], chunks[n:]
    received = [lax.ppermute(c, ("group", "dp"), split_swaps) for c in sent]
    done, returned = [], []
    for i in range(n):
        kept, back = work(widths[i], own[i], received[i])
        done.append(kept)
        returned.append(lax.ppermute(back, ("group", "dp"), split_swaps))
    out = place(True, firsts, done)
    for i in range(n):
        if i == n - 1:
            out = whole(own_block, whole_received.reshape(rows, both), out)
        out = place(False, [firsts[i]], [returned[i]], out)
    return out.reshape(operands.shape)


def solution(mesh):
    spec = P("group", "dp", None, None)
    return jax.shard_map(local, mesh=mesh, in_specs=(spec,), out_specs=spec, check_vma=False)
```

```python
import functools

import jax
import jax.numpy as jnp
from jax import lax
from jax.experimental import pallas as pl
from jax.experimental.pallas import tpu as pltpu
from jax.sharding import PartitionSpec as P

HEAD = 256
HEADS = 8
INNER = HEAD * HEADS
KEPT = INNER // 2
CHUNKS = (3, 1)
TOGETHER = 4
FACTOR = HEAD ** (-0.5)
PARAMS = pltpu.CompilerParams(vmem_limit_bytes=12 * 1024 * 1024)

VMEM = pl.BlockSpec(memory_space=pltpu.VMEM)
ANY = pl.BlockSpec(memory_space=pl.ANY)
HBM = pl.BlockSpec(memory_space=pltpu.HBM)


def dot(a, b, dims):
    return lax.dot_general(a, b, (dims, ((), ())), preferred_element_type=jnp.float32)


def softmax(scores, axis):
    exponent = jnp.exp(scores - jnp.max(scores, axis=axis, keepdims=True))
    return exponent / jnp.sum(exponent, axis=axis, keepdims=True)


def decoder_half(query, out_grad, key, value):
    scores = dot(query, key, ((1,), (1,))) * FACTOR
    grad_weights = dot(out_grad, value, ((1,), (1,)))
    yield
    weights = softmax(scores, -1)
    weights_b = weights.astype(jnp.bfloat16)
    yield
    attended = dot(weights_b, value, ((1,), (0,)))
    yield
    row_delta = jnp.sum(out_grad.astype(jnp.float32) * attended, axis=-1, keepdims=True)
    grad_scores = (weights * (grad_weights - row_delta) * FACTOR).astype(jnp.bfloat16)
    yield
    query_grad = dot(grad_scores, key, ((1,), (0,)))
    return attended.astype(jnp.bfloat16), query_grad.astype(jnp.bfloat16), weights_b, grad_scores


def encoder_half(query, out_grad, key, value):
    scores = dot(key, query, ((1,), (1,))) * FACTOR
    grad_weights = dot(value, out_grad, ((1,), (1,)))
    yield
    weights = softmax(scores, 0)
    weights_b = weights.astype(jnp.bfloat16)
    yield
    value_grad = dot(weights_b, out_grad, ((1,), (0,)))
    row_delta = jnp.sum(weights_b.astype(jnp.float32) * grad_weights, axis=0, keepdims=True)
    grad_scores = (weights * (grad_weights - row_delta) * FACTOR).astype(jnp.bfloat16)
    yield
    key_grad = dot(grad_scores, query, ((1,), (0,)))
    return key_grad.astype(jnp.bfloat16), value_grad.astype(jnp.bfloat16)


def head_work(query, out_grad, key, value):
    attended, query_grad, weights_b, grad_scores = yield from decoder_half(query, out_grad, key, value)
    yield
    key_grad = dot(grad_scores, query, ((0,), (0,))).astype(jnp.bfloat16)
    value_grad = dot(weights_b, out_grad, ((0,), (0,))).astype(jnp.bfloat16)
    return attended, query_grad, key_grad, value_grad


def side_by_side(heads):
    results = [None] * len(heads)
    left = list(range(len(heads)))
    while left:
        for i in list(left):
            try:
                next(heads[i])
            except StopIteration as end:
                results[i] = end.value
                left.remove(i)
    return results


def on_decoder():
    return lax.axis_index("group") == 1


def in_split_plan():
    return lax.rem(lax.axis_index("dp"), 2) == 0


def side(kept):
    role = lax.axis_index("group")
    return role if kept else 1 - role


def views(block, at, width):
    return [block.at[:, pl.ds(pl.multiple_of(i * INNER + at, HEAD), width)] for i in range(2)]


def run_copies(copies):
    for copy in copies:
        copy.start()
    for copy in copies:
        copy.wait()


def half_copies(block, at, chunk, sems):
    parts = views(block, at, chunk.shape[-1])
    return [pltpu.make_async_copy(view, chunk.at[j], sems.at[j]) for j, view in enumerate(parts)]


def first_kernel(block, head, sent, sems):
    split = in_split_plan()
    pl.when(split)(lambda: run_copies(half_copies(block, side(False) * KEPT, sent, sems)))
    pl.when(jnp.logical_not(split))(lambda: run_copies(half_copies(block, 0, head, sems)))


def second_kernel(block, _, others, own_block, kept, sems):
    split = in_split_plan()

    def whole():
        copies = half_copies(block, HEAD, others, sems)
        run_copies(copies + [pltpu.make_async_copy(block, own_block, sems.at[2])])

    pl.when(split)(lambda: run_copies(half_copies(block, side(True) * KEPT, kept, sems)))
    pl.when(jnp.logical_not(split))(whole)


def work_kernel(own, received, kept, *backs):
    def run(decoder):
        query_side, key_side = (own, received) if decoder else (received, own)
        cols = [slice(h * HEAD, (h + 1) * HEAD) for h in range(HEADS // 2)]
        heads = [
            head_work(query_side[0, :, c], query_side[1, :, c], key_side[0, :, c], key_side[1, :, c]) for c in cols
        ]
        places = [(back, i) for back in backs for i in range(back.shape[-1] // HEAD)]
        for c, (back, i), result in zip(cols, places, side_by_side(heads)):
            front, rear = result[:2], result[2:]
            stay, go = (front, rear) if decoder else (rear, front)
            for j in range(2):
                kept[j, :, c] = stay[j]
                back[j, :, i * HEAD : (i + 1) * HEAD] = go[j]

    split = in_split_plan()
    pl.when(jnp.logical_and(split, on_decoder()))(lambda: run(True))
    pl.when(jnp.logical_and(split, jnp.logical_not(on_decoder())))(lambda: run(False))


def whole_kernel(first, own, received, _, out, stage, sems):
    def run(decoder):
        def partner(h, i):
            if first:
                return received[0 if decoder else 1, i]
            return received[i, :, (h - 1) * HEAD : h * HEAD]

        copies = []
        todo = range(1) if first else range(1, HEADS)
        for start in range(0, len(todo), TOGETHER):
            heads = todo[start : start + TOGETHER]
            cols = {h: [slice(i * INNER + h * HEAD, i * INNER + (h + 1) * HEAD) for i in range(2)] for h in heads}
            work = decoder_half if decoder else encoder_half
            mine = {h: [own[:, c] for c in cols[h]] for h in heads}
            theirs = {h: [partner(h, i) for i in range(2)] for h in heads}
            sides = (mine, theirs) if decoder else (theirs, mine)
            results = side_by_side([work(*sides[0][h], *sides[1][h]) for h in heads])
            for h, result in zip(heads, results):
                for i in range(2):
                    stage[h, i] = result[i]
                    copies.append(pltpu.make_async_copy(stage.at[h, i], out.at[:, cols[h][i]], sems.at[h, i]))
                    copies[-1].start()
        for copy in copies:
            copy.wait()

    whole = jnp.logical_not(in_split_plan())
    pl.when(jnp.logical_and(whole, on_decoder()))(lambda: run(True))
    pl.when(jnp.logical_and(whole, jnp.logical_not(on_decoder())))(lambda: run(False))


def place_kernel(kept, firsts, aliased, *rest):
    *chunks, out, sems = rest
    if aliased:
        chunks = chunks[:-1]

    def run():
        copies = []
        for i, (first, chunk) in enumerate(zip(firsts, chunks)):
            for j, view in enumerate(views(out, side(kept) * KEPT + first, chunk.shape[-1])):
                copies.append(pltpu.make_async_copy(chunk.at[j], view, sems.at[i, j]))
        run_copies(copies)

    pl.when(in_split_plan())(run)


def cost(moved, flops=0, exps=0):
    return pl.CostEstimate(flops=flops, bytes_accessed=moved, transcendentals=exps)


def local(operands):
    rows, both = operands.shape[2:]
    count = lax.axis_size("dp")
    swaps = [(i, (i + count) % (2 * count)) for i in range(2 * count)]
    split_swaps = [p for p in swaps if p[0] % 2 == 0]
    whole_swaps = [p for p in swaps if p[0] % 2 == 1]
    widths = [n * HEAD for n in CHUNKS]
    firsts = [sum(widths[:i]) for i in range(len(widths))]
    n = len(widths)
    half, head, others = (2, rows, KEPT), (2, rows, HEAD), (2, rows, INNER - HEAD)

    def nothing(shape):
        return pl.pallas_call(
            lambda out: None,
            out_shape=pltpu.VMEM(shape, jnp.bfloat16),
            out_specs=VMEM,
            compiler_params=PARAMS,
            cost_estimate=cost(0),
            name="nothing",
        )()

    def load(kernel, shapes, name, *after):
        return pl.pallas_call(
            kernel,
            out_shape=[pltpu.VMEM(shape, jnp.bfloat16) for shape in shapes],
            in_specs=[HBM] + [ANY] * len(after),
            out_specs=[VMEM] * len(shapes),
            scratch_shapes=[pltpu.SemaphoreType.DMA((3,))],
            compiler_params=PARAMS,
            cost_estimate=cost(0),
            name=name,
        )(block, *after)

    def work(own, received):
        return pl.pallas_call(
            work_kernel,
            out_shape=[jax.ShapeDtypeStruct((2, rows, width), jnp.bfloat16) for width in [KEPT, *widths]],
            in_specs=[VMEM, VMEM],
            out_specs=[VMEM] * (1 + n),
            compiler_params=PARAMS,
            cost_estimate=cost(0, flops=12 * rows * rows * KEPT, exps=rows * KEPT),
            name="work",
        )(own, received)

    def place(kept, at, chunks, out=None):
        extra = [] if out is None else [out]
        return pl.pallas_call(
            functools.partial(place_kernel, kept, at, bool(extra)),
            out_shape=jax.ShapeDtypeStruct((rows, both), jnp.bfloat16),
            in_specs=[VMEM] * len(chunks) + [ANY] * len(extra),
            out_specs=ANY,
            scratch_shapes=[pltpu.SemaphoreType.DMA((len(chunks), 2))],
            input_output_aliases={len(chunks): 0} if extra else {},
            compiler_params=PARAMS,
            cost_estimate=cost(0),
            name="place",
        )(*chunks, *extra)

    def whole(first, own, received, out):
        return pl.pallas_call(
            functools.partial(whole_kernel, first),
            out_shape=jax.ShapeDtypeStruct((rows, both), jnp.bfloat16),
            in_specs=[VMEM, VMEM, ANY],
            out_specs=ANY,
            scratch_shapes=[
                pltpu.VMEM((HEADS, 2, rows, HEAD), jnp.bfloat16),
                pltpu.SemaphoreType.DMA((HEADS, 2)),
            ],
            input_output_aliases={2: 0},
            compiler_params=PARAMS,
            cost_estimate=cost(0),
            name="whole",
        )(own, received, out)

    block = pltpu.with_memory_space_constraint(operands.reshape(rows, both), pltpu.HBM)
    first_head, sent = load(first_kernel, [head, half], "first")
    gathered = lax.cond(
        in_split_plan(),
        lambda chunk: nothing((2, *head)),
        lambda chunk: lax.all_gather(chunk, "group"),
        first_head,
    )
    gathered, sent = lax.optimization_barrier((gathered, sent))
    received = lax.ppermute(sent, ("group", "dp"), split_swaps)
    other_heads, own_block, own = load(second_kernel, [others, (rows, both), half], "second", gathered)
    whole_received = lax.ppermute(other_heads, ("group", "dp"), whole_swaps)
    kept, *backs = work(own, received)
    returned = [lax.ppermute(back, ("group", "dp"), split_swaps) for back in backs]
    out = place(True, [0], [kept])
    out = whole(True, own_block, gathered, out)
    for i in range(n):
        if i == n - 1:
            out = whole(False, own_block, whole_received, out)
        out = place(False, [firsts[i]], [returned[i]], out)
    return out.reshape(operands.shape)


def solution(mesh):
    spec = P("group", "dp", None, None)
    return jax.shard_map(local, mesh=mesh, in_specs=(spec,), out_specs=spec, check_vma=False)
```

```python
import functools

import jax
import jax.numpy as jnp
from jax import lax
from jax.experimental import pallas as pl
from jax.experimental.pallas import tpu as pltpu
from jax.sharding import PartitionSpec as P

HEAD = 256
HEADS = 8
INNER = HEAD * HEADS
KEPT = INNER // 2
CHUNKS = (3, 1)
TOGETHER = 4
EARLY = (2 * HEAD, HEAD + HEAD // 2)
FACTOR = HEAD ** (-0.5)
PARAMS = pltpu.CompilerParams(vmem_limit_bytes=12 * 1024 * 1024)

VMEM = pl.BlockSpec(memory_space=pltpu.VMEM)
ANY = pl.BlockSpec(memory_space=pl.ANY)
HBM = pl.BlockSpec(memory_space=pltpu.HBM)


def dot(a, b, dims):
    return lax.dot_general(a, b, (dims, ((), ())), preferred_element_type=jnp.float32)


def softmax(scores, axis):
    exponent = jnp.exp(scores - jnp.max(scores, axis=axis, keepdims=True))
    return exponent / jnp.sum(exponent, axis=axis, keepdims=True)


def decoder_half(query, out_grad, key, value):
    scores = dot(query, key, ((1,), (1,))) * FACTOR
    grad_weights = dot(out_grad, value, ((1,), (1,)))
    yield
    weights = softmax(scores, -1)
    weights_b = weights.astype(jnp.bfloat16)
    yield
    attended = dot(weights_b, value, ((1,), (0,)))
    yield
    row_delta = jnp.sum(out_grad.astype(jnp.float32) * attended, axis=-1, keepdims=True)
    grad_scores = (weights * (grad_weights - row_delta) * FACTOR).astype(jnp.bfloat16)
    yield
    query_grad = dot(grad_scores, key, ((1,), (0,)))
    return attended.astype(jnp.bfloat16), query_grad.astype(jnp.bfloat16), weights_b, grad_scores


def encoder_half(query, out_grad, key, value):
    scores = dot(key, query, ((1,), (1,))) * FACTOR
    grad_weights = dot(value, out_grad, ((1,), (1,)))
    yield
    weights = softmax(scores, 0)
    weights_b = weights.astype(jnp.bfloat16)
    yield
    value_grad = dot(weights_b, out_grad, ((1,), (0,)))
    row_delta = jnp.sum(weights_b.astype(jnp.float32) * grad_weights, axis=0, keepdims=True)
    grad_scores = (weights * (grad_weights - row_delta) * FACTOR).astype(jnp.bfloat16)
    yield
    key_grad = dot(grad_scores, query, ((1,), (0,)))
    return key_grad.astype(jnp.bfloat16), value_grad.astype(jnp.bfloat16)


def head_work(query, out_grad, key, value):
    attended, query_grad, weights_b, grad_scores = yield from decoder_half(query, out_grad, key, value)
    yield
    key_grad = dot(grad_scores, query, ((0,), (0,))).astype(jnp.bfloat16)
    value_grad = dot(weights_b, out_grad, ((0,), (0,))).astype(jnp.bfloat16)
    return attended, query_grad, key_grad, value_grad


def side_by_side(heads):
    results = [None] * len(heads)
    left = list(range(len(heads)))
    while left:
        for i in list(left):
            try:
                next(heads[i])
            except StopIteration as end:
                results[i] = end.value
                left.remove(i)
    return results


def on_decoder():
    return lax.axis_index("group") == 1


def in_split_plan():
    return lax.rem(lax.axis_index("dp"), 2) == 0


def side(kept):
    role = lax.axis_index("group")
    return role if kept else 1 - role


def views(block, at, width):
    return [block.at[:, pl.ds(pl.multiple_of(i * INNER + at, HEAD), width)] for i in range(2)]


def run_copies(copies):
    for copy in copies:
        copy.start()
    for copy in copies:
        copy.wait()


def half_copies(block, at, chunk, sems):
    parts = views(block, at, chunk.shape[-1])
    return [pltpu.make_async_copy(view, chunk.at[j], sems.at[j]) for j, view in enumerate(parts)]


def first_kernel(block, early, sent, sems):
    split = in_split_plan()

    def whole():
        copies = []
        for i, (to, count) in enumerate(((0, EARLY[0]), (EARLY[0], EARLY[1]))):
            part = block.at[:, i * INNER : i * INNER + count]
            copies.append(pltpu.make_async_copy(part, early.at[:, to : to + count], sems.at[i]))
        run_copies(copies)

    pl.when(split)(lambda: run_copies(half_copies(block, side(False) * KEPT, sent, sems)))
    pl.when(jnp.logical_not(split))(whole)


def second_kernel(block, _, others, own_block, kept, sems):
    split = in_split_plan()

    def whole():
        copies = [pltpu.make_async_copy(block, own_block, sems.at[2])]
        for i, to in enumerate((0, INNER - EARLY[0])):
            part = block.at[:, i * INNER + EARLY[i] : (i + 1) * INNER]
            copies.append(pltpu.make_async_copy(part, others.at[:, to : to + INNER - EARLY[i]], sems.at[i]))
        run_copies(copies)

    pl.when(split)(lambda: run_copies(half_copies(block, side(True) * KEPT, kept, sems)))
    pl.when(jnp.logical_not(split))(whole)


def work_kernel(own, received, out, *rest):
    *backs, kept, sems = rest

    def run(decoder):
        query_side, key_side = (own, received) if decoder else (received, own)
        cols = [slice(h * HEAD, (h + 1) * HEAD) for h in range(HEADS // 2)]
        heads = [
            head_work(query_side[0, :, c], query_side[1, :, c], key_side[0, :, c], key_side[1, :, c]) for c in cols
        ]
        places = [(back, i) for back in backs for i in range(back.shape[-1] // HEAD)]
        for c, (back, i), result in zip(cols, places, side_by_side(heads)):
            front, rear = result[:2], result[2:]
            stay, go = (front, rear) if decoder else (rear, front)
            for j in range(2):
                kept[j, :, c] = stay[j]
                back[j, :, i * HEAD : (i + 1) * HEAD] = go[j]
        parts = views(out, side(True) * KEPT, KEPT)
        run_copies([pltpu.make_async_copy(kept.at[j], view, sems.at[j]) for j, view in enumerate(parts)])

    split = in_split_plan()
    pl.when(jnp.logical_and(split, on_decoder()))(lambda: run(True))
    pl.when(jnp.logical_and(split, jnp.logical_not(on_decoder())))(lambda: run(False))


def whole_kernel(first, own, *rest):
    gathered, *received, _, out, stage, sems = rest

    def run(decoder):
        def partner(h, i):
            start, end, early = h * HEAD, (h + 1) * HEAD, EARLY[i]
            parts = []
            if start < early:
                at = i * EARLY[0]
                parts.append(gathered[0 if decoder else 1, :, at + start : at + min(end, early)])
            if end > early:
                at = i * (INNER - EARLY[0]) - early
                parts.append(received[0][:, at + max(start, early) : at + end])
            return parts[0] if len(parts) == 1 else jnp.concatenate(parts, axis=1)

        copies = []
        todo = range(1) if first else range(1, HEADS)
        for start in range(0, len(todo), TOGETHER):
            heads = todo[start : start + TOGETHER]
            cols = {h: [slice(i * INNER + h * HEAD, i * INNER + (h + 1) * HEAD) for i in range(2)] for h in heads}
            work = decoder_half if decoder else encoder_half
            mine = {h: [own[:, c] for c in cols[h]] for h in heads}
            theirs = {h: [partner(h, i) for i in range(2)] for h in heads}
            sides = (mine, theirs) if decoder else (theirs, mine)
            results = side_by_side([work(*sides[0][h], *sides[1][h]) for h in heads])
            for h, result in zip(heads, results):
                for i in range(2):
                    stage[h, i] = result[i]
                    copies.append(pltpu.make_async_copy(stage.at[h, i], out.at[:, cols[h][i]], sems.at[h, i]))
                    copies[-1].start()
        for copy in copies:
            copy.wait()

    whole = jnp.logical_not(in_split_plan())
    pl.when(jnp.logical_and(whole, on_decoder()))(lambda: run(True))
    pl.when(jnp.logical_and(whole, jnp.logical_not(on_decoder())))(lambda: run(False))


def place_kernel(first, chunk, _, out, sems):
    def run():
        parts = views(out, side(False) * KEPT + first, chunk.shape[-1])
        run_copies([pltpu.make_async_copy(chunk.at[j], view, sems.at[j]) for j, view in enumerate(parts)])

    pl.when(in_split_plan())(run)


def cost(moved, flops=0, exps=0):
    return pl.CostEstimate(flops=flops, bytes_accessed=moved, transcendentals=exps)


def local(operands):
    rows, both = operands.shape[2:]
    count = lax.axis_size("dp")
    swaps = [(i, (i + count) % (2 * count)) for i in range(2 * count)]
    split_swaps = [p for p in swaps if p[0] % 2 == 0]
    whole_swaps = [p for p in swaps if p[0] % 2 == 1]
    widths = [n * HEAD for n in CHUNKS]
    firsts = [sum(widths[:i]) for i in range(len(widths))]
    n = len(widths)
    half, early, others = (2, rows, KEPT), (rows, sum(EARLY)), (rows, both - sum(EARLY))

    def nothing(shape):
        return pl.pallas_call(
            lambda out: None,
            out_shape=pltpu.VMEM(shape, jnp.bfloat16),
            out_specs=VMEM,
            compiler_params=PARAMS,
            cost_estimate=cost(0),
            name="nothing",
        )()

    def load(kernel, shapes, name, *after):
        return pl.pallas_call(
            kernel,
            out_shape=[pltpu.VMEM(shape, jnp.bfloat16) for shape in shapes],
            in_specs=[HBM] + [ANY] * len(after),
            out_specs=[VMEM] * len(shapes),
            scratch_shapes=[pltpu.SemaphoreType.DMA((3,))],
            compiler_params=PARAMS,
            cost_estimate=cost(0),
            name=name,
        )(block, *after)

    def work(own, received):
        return pl.pallas_call(
            work_kernel,
            out_shape=[jax.ShapeDtypeStruct((rows, both), jnp.bfloat16)]
            + [jax.ShapeDtypeStruct((2, rows, width), jnp.bfloat16) for width in widths],
            in_specs=[VMEM, VMEM],
            out_specs=[ANY] + [VMEM] * n,
            scratch_shapes=[pltpu.VMEM(half, jnp.bfloat16), pltpu.SemaphoreType.DMA((2,))],
            compiler_params=PARAMS,
            cost_estimate=cost(0, flops=12 * rows * rows * KEPT, exps=rows * KEPT),
            name="work",
        )(own, received)

    def place(first, chunk, out):
        return pl.pallas_call(
            functools.partial(place_kernel, first),
            out_shape=jax.ShapeDtypeStruct((rows, both), jnp.bfloat16),
            in_specs=[VMEM, ANY],
            out_specs=ANY,
            scratch_shapes=[pltpu.SemaphoreType.DMA((2,))],
            input_output_aliases={1: 0},
            compiler_params=PARAMS,
            cost_estimate=cost(0),
            name="place",
        )(chunk, out)

    def whole(first, own, received, out):
        return pl.pallas_call(
            functools.partial(whole_kernel, first),
            out_shape=jax.ShapeDtypeStruct((rows, both), jnp.bfloat16),
            in_specs=[VMEM] * (1 + len(received)) + [ANY],
            out_specs=ANY,
            scratch_shapes=[
                pltpu.VMEM((HEADS, 2, rows, HEAD), jnp.bfloat16),
                pltpu.SemaphoreType.DMA((HEADS, 2)),
            ],
            input_output_aliases={1 + len(received): 0},
            compiler_params=PARAMS,
            cost_estimate=cost(0),
            name="whole",
        )(own, *received, out)

    block = pltpu.with_memory_space_constraint(operands.reshape(rows, both), pltpu.HBM)
    first_columns, sent = load(first_kernel, [early, half], "first")
    gathered = lax.cond(
        in_split_plan(),
        lambda chunk: nothing((2, *early)),
        lambda chunk: lax.all_gather(chunk, "group"),
        first_columns,
    )
    gathered, sent = lax.optimization_barrier((gathered, sent))
    received = lax.ppermute(sent, ("group", "dp"), split_swaps)
    other_columns, own_block, own = load(second_kernel, [others, (rows, both), half], "second", gathered)
    whole_received = lax.ppermute(other_columns, ("group", "dp"), whole_swaps)
    out, *backs = work(own, received)
    returned = [lax.ppermute(back, ("group", "dp"), split_swaps) for back in backs]
    out = whole(True, own_block, [gathered], out)
    for i in range(n):
        if i == n - 1:
            out = whole(False, own_block, [gathered, whole_received], out)
        out = place(firsts[i], returned[i], out)
    return out.reshape(operands.shape)


def solution(mesh):
    spec = P("group", "dp", None, None)
    return jax.shard_map(local, mesh=mesh, in_specs=(spec,), out_specs=spec, check_vma=False)
```

```python
import functools

import jax
import jax.numpy as jnp
from jax import lax
from jax.experimental import pallas as pl
from jax.experimental.pallas import tpu as pltpu
from jax.sharding import PartitionSpec as P

HEAD = 256
HEADS = 8
INNER = HEAD * HEADS
KEPT = INNER // 2
CHUNKS = (2, 1, 1)
TOGETHER = 4
FACTOR = HEAD ** (-0.5)
PARAMS = pltpu.CompilerParams(vmem_limit_bytes=12 * 1024 * 1024)

VMEM = pl.BlockSpec(memory_space=pltpu.VMEM)
ANY = pl.BlockSpec(memory_space=pl.ANY)
HBM = pl.BlockSpec(memory_space=pltpu.HBM)


def dot(a, b, dims):
    return lax.dot_general(a, b, (dims, ((), ())), preferred_element_type=jnp.float32)


def softmax(scores, axis):
    exponent = jnp.exp(scores - jnp.max(scores, axis=axis, keepdims=True))
    return exponent / jnp.sum(exponent, axis=axis, keepdims=True)


def decoder_half(query, out_grad, key, value):
    scores = dot(query, key, ((1,), (1,))) * FACTOR
    grad_weights = dot(out_grad, value, ((1,), (1,)))
    yield
    weights = softmax(scores, -1)
    weights_b = weights.astype(jnp.bfloat16)
    yield
    attended = dot(weights_b, value, ((1,), (0,)))
    yield
    row_delta = jnp.sum(out_grad.astype(jnp.float32) * attended, axis=-1, keepdims=True)
    grad_scores = (weights * (grad_weights - row_delta) * FACTOR).astype(jnp.bfloat16)
    yield
    query_grad = dot(grad_scores, key, ((1,), (0,)))
    return attended.astype(jnp.bfloat16), query_grad.astype(jnp.bfloat16), weights_b, grad_scores


def encoder_half(query, out_grad, key, value):
    scores = dot(key, query, ((1,), (1,))) * FACTOR
    grad_weights = dot(value, out_grad, ((1,), (1,)))
    yield
    weights = softmax(scores, 0)
    weights_b = weights.astype(jnp.bfloat16)
    yield
    value_grad = dot(weights_b, out_grad, ((1,), (0,)))
    row_delta = jnp.sum(weights_b.astype(jnp.float32) * grad_weights, axis=0, keepdims=True)
    grad_scores = (weights * (grad_weights - row_delta) * FACTOR).astype(jnp.bfloat16)
    yield
    key_grad = dot(grad_scores, query, ((1,), (0,)))
    return key_grad.astype(jnp.bfloat16), value_grad.astype(jnp.bfloat16)


def head_work(query, out_grad, key, value):
    attended, query_grad, weights_b, grad_scores = yield from decoder_half(query, out_grad, key, value)
    yield
    key_grad = dot(grad_scores, query, ((0,), (0,))).astype(jnp.bfloat16)
    value_grad = dot(weights_b, out_grad, ((0,), (0,))).astype(jnp.bfloat16)
    return attended, query_grad, key_grad, value_grad


def side_by_side(heads):
    results = [None] * len(heads)
    left = list(range(len(heads)))
    while left:
        for i in list(left):
            try:
                next(heads[i])
            except StopIteration as end:
                results[i] = end.value
                left.remove(i)
    return results


def on_decoder():
    return lax.axis_index("group") == 1


def in_split_plan():
    return lax.rem(lax.axis_index("dp"), 2) == 0


def side(kept):
    role = lax.axis_index("group")
    return role if kept else 1 - role


def views(block, at, width):
    return [block.at[:, pl.ds(pl.multiple_of(i * INNER + at, HEAD), width)] for i in range(2)]


def run_copies(copies):
    for copy in copies:
        copy.start()
    for copy in copies:
        copy.wait()


def load_kernel(parts, block, *rest):
    *chunks, whole, sems = rest

    def split():
        copies = []
        for i, ((kept, first), chunk) in enumerate(zip(parts, chunks)):
            for j, view in enumerate(views(block, side(kept) * KEPT + first, chunk.shape[-1])):
                copies.append(pltpu.make_async_copy(view, chunk.at[j], sems.at[i, j]))
        run_copies(copies)

    def all_of_it():
        run_copies([pltpu.make_async_copy(block, whole, sems.at[0, 0])])

    pl.when(in_split_plan())(split)
    pl.when(jnp.logical_not(in_split_plan()))(all_of_it)


def work_kernel(width, own, received, kept, back):
    def run(decoder):
        query_side, key_side = (own, received) if decoder else (received, own)
        front, rear = (kept, back) if decoder else (back, kept)
        cols = [slice(h * HEAD, (h + 1) * HEAD) for h in range(width // HEAD)]
        heads = [
            head_work(query_side[0, :, c], query_side[1, :, c], key_side[0, :, c], key_side[1, :, c]) for c in cols
        ]
        for c, (attended, query_grad, key_grad, value_grad) in zip(cols, side_by_side(heads)):
            front[0, :, c] = attended
            front[1, :, c] = query_grad
            rear[0, :, c] = key_grad
            rear[1, :, c] = value_grad

    split = in_split_plan()
    pl.when(jnp.logical_and(split, on_decoder()))(lambda: run(True))
    pl.when(jnp.logical_and(split, jnp.logical_not(on_decoder())))(lambda: run(False))


def whole_kernel(own, received, _, out, stage, sems):
    def run(decoder):
        query_side, key_side = (own, received) if decoder else (received, own)
        copies = []
        for start in range(0, HEADS, TOGETHER):
            heads = range(start, start + TOGETHER)
            cols = {h: [slice(i * INNER + h * HEAD, i * INNER + (h + 1) * HEAD) for i in range(2)] for h in heads}
            work = decoder_half if decoder else encoder_half
            results = side_by_side([work(*[ref[:, c] for ref in (query_side, key_side) for c in cols[h]]) for h in heads])
            for h, result in zip(heads, results):
                for i in range(2):
                    stage[h, i] = result[i]
                    copies.append(pltpu.make_async_copy(stage.at[h, i], out.at[:, cols[h][i]], sems.at[h, i]))
                    copies[-1].start()
        for copy in copies:
            copy.wait()

    whole = jnp.logical_not(in_split_plan())
    pl.when(jnp.logical_and(whole, on_decoder()))(lambda: run(True))
    pl.when(jnp.logical_and(whole, jnp.logical_not(on_decoder())))(lambda: run(False))


def place_kernel(kept, firsts, aliased, *rest):
    *chunks, out, sems = rest
    if aliased:
        chunks = chunks[:-1]

    def run():
        copies = []
        for i, (first, chunk) in enumerate(zip(firsts, chunks)):
            for j, view in enumerate(views(out, side(kept) * KEPT + first, chunk.shape[-1])):
                copies.append(pltpu.make_async_copy(chunk.at[j], view, sems.at[i, j]))
        run_copies(copies)

    pl.when(in_split_plan())(run)


def cost(moved, flops=0, exps=0):
    return pl.CostEstimate(flops=flops, bytes_accessed=moved, transcendentals=exps)


def local(operands):
    rows, both = operands.shape[2:]
    count = lax.axis_size("dp")
    swaps = [(i, (i + count) % (2 * count)) for i in range(2 * count)]
    split_swaps = [p for p in swaps if p[0] % 2 == 0]
    whole_swaps = [p for p in swaps if p[0] % 2 == 1]
    widths = [n * HEAD for n in CHUNKS]
    firsts = [sum(widths[:i]) for i in range(len(widths))]
    n = len(widths)

    def load(block, parts):
        return pl.pallas_call(
            functools.partial(load_kernel, [(kept, firsts[i]) for kept, i in parts]),
            out_shape=[pltpu.VMEM((2, rows, widths[i]), jnp.bfloat16) for _, i in parts]
            + [pltpu.VMEM((rows, both), jnp.bfloat16)],
            in_specs=[HBM],
            out_specs=[VMEM] * (len(parts) + 1),
            scratch_shapes=[pltpu.SemaphoreType.DMA((len(parts), 2))],
            compiler_params=PARAMS,
            cost_estimate=cost(0),
            name="load",
        )(block)

    def work(width, own, received):
        return pl.pallas_call(
            functools.partial(work_kernel, width),
            out_shape=[jax.ShapeDtypeStruct((2, rows, width), jnp.bfloat16)] * 2,
            in_specs=[VMEM, VMEM],
            out_specs=[VMEM, VMEM],
            compiler_params=PARAMS,
            cost_estimate=cost(0, flops=12 * rows * rows * width, exps=rows * width),
            name="work",
        )(own, received)

    def place(kept, at, chunks, out=None):
        extra = [] if out is None else [out]
        return pl.pallas_call(
            functools.partial(place_kernel, kept, at, bool(extra)),
            out_shape=jax.ShapeDtypeStruct((rows, both), jnp.bfloat16),
            in_specs=[VMEM] * len(chunks) + [ANY] * len(extra),
            out_specs=ANY,
            scratch_shapes=[pltpu.SemaphoreType.DMA((len(chunks), 2))],
            input_output_aliases={len(chunks): 0} if extra else {},
            compiler_params=PARAMS,
            cost_estimate=cost(0),
            name="place",
        )(*chunks, *extra)

    def whole(own, received, out):
        return pl.pallas_call(
            whole_kernel,
            out_shape=jax.ShapeDtypeStruct((rows, both), jnp.bfloat16),
            in_specs=[VMEM, VMEM, ANY],
            out_specs=ANY,
            scratch_shapes=[
                pltpu.VMEM((HEADS, 2, rows, HEAD), jnp.bfloat16),
                pltpu.SemaphoreType.DMA((HEADS, 2)),
            ],
            input_output_aliases={2: 0},
            compiler_params=PARAMS,
            cost_estimate=cost(0),
            name="whole",
        )(own, received, out)

    whole_received = lax.ppermute(operands, ("group", "dp"), whole_swaps)
    block = pltpu.with_memory_space_constraint(operands.reshape(rows, both), pltpu.HBM)
    *chunks, own_block = load(block, [(True, i) for i in range(n)] + [(False, i) for i in range(n)])
    own, sent = chunks[:n], chunks[n:]
    received = [lax.ppermute(c, ("group", "dp"), split_swaps) for c in sent]
    done, returned = [], []
    for i in range(n):
        kept, back = work(widths[i], own[i], received[i])
        done.append(kept)
        returned.append(lax.ppermute(back, ("group", "dp"), split_swaps))
    out = place(True, firsts, done)
    for i in range(n):
        if i == n - 1:
            out = whole(own_block, whole_received.reshape(rows, both), out)
        out = place(False, [firsts[i]], [returned[i]], out)
    return out.reshape(operands.shape)


def solution(mesh):
    spec = P("group", "dp", None, None)
    return jax.shard_map(local, mesh=mesh, in_specs=(spec,), out_specs=spec, check_vma=False)
```
